32 devices in a mesh: tile: 32 (over z, y, x, core), real: 1.
Axes of the slice: x: 2, y: 2, z: 4, core: 2. Of those that a mesh axis runs over, the one named last changes fastest.
Arguments:
- voltage: float32 [32, 32768], P('real', 'tile'), may hold values from -4 to 4
- recovery: float32 [32, 32768], P('real', 'tile'), may hold values from -3 to 3
- increments: float32 [10, 32, 32768], P(None, 'real', 'tile'), may hold values from -6 to 6
- band_weight: bfloat16 [32768, 3072], P('tile'), may hold values from -0.125 to 0.125
- time_scale: float32 [32768], P('tile'), may hold values from 0.05 to 0.5
- tract_in: bfloat16 [4, 32768, 256], P(None, 'tile'), may hold values from -0.375 to 0.375
- tract_out: bfloat16 [4, 32768, 256], P(None, 'tile'), may hold values from -0.1875 to 0.1875
- matching_masks: int32 [4], replicated, may hold values from 1 to 31, as said below
- tract_on: int32 [32, 4], P('tile'), may hold values 0 or 1
Outputs:
- voltage_end: float32 [32, 32768], P('real', 'tile')
- recovery_end: float32 [32, 32768], P('real', 'tile')
The draws below stay inside these ranges and needn't reach their ends.
Inputs may be any that keep to these rules, and one draw needn't show every extreme that they name: `matching_masks`: the 4 masks are distinct.
All inputs are finite; a program needn't handle non-finite values. No bound on the sum of `tract_on` on one device may be relied on, other than what follows from the above.
Results may differ from the reference program's by a relative error of at most 0.0013.
Values may be sent and summed in bfloat16 or wider, within the bound.
A program may use at most 64 MiB of HBM per device.

```python
import math
import jax
import jax.numpy as jnp
from jax import lax

R = 32
TILE_V = 1024
HW = 1024
RANK = 256
MATCH = 4
STEPS = 10
TILES = 32
VERTS = 32768


def draw_matching_masks(key, part):
    return (jax.random.permutation(key, TILES - 1)[:MATCH] + 1).astype(jnp.int32)


def with_ends(result, stream_key, low, high):
    shape = result.shape
    spot = [jax.random.randint(jax.random.fold_in(stream_key, axis), (), 0, shape[axis]) for axis in range(len(shape))]
    result = result.at[tuple(spot)].set(low)
    longest = shape.index(max(shape))
    spot[longest] = (spot[longest] + 1) % shape[longest]
    return result.at[tuple(spot)].set(high)


def block_scale(own_key, extent, split, least, largest):
    def one(dim, shards_of):
        heights = jax.random.uniform(jax.random.fold_in(jax.random.fold_in(own_key, 6), dim), (shards_of,), jnp.float32, least / len(split), largest / len(split))
        return jnp.repeat(jnp.exp(heights), extent[dim] // shards_of).reshape((-1,) + (1,) * (len(extent) - dim - 1))

    level = one(*split[0])
    for cut in split[1:]:
        level = level * one(*cut)
    return level


def bell_draw(stream_key, shape, width, bound, shards=(), held_as=jnp.bfloat16):
    values = width * jax.random.normal(stream_key, shape, jnp.float32)
    if shards:
        values = values * block_scale(stream_key, shape, shards, -0.22, 0.18)
    return jnp.clip(values, -bound, bound).astype(held_as)


def setup_inputs(seed: int = 0, part: int = 0) -> dict:
    key_list = jax.random.split(jax.random.key(seed), 10)
    part_keys = jax.random.split(jax.random.fold_in(key_list[9], part), 10)
    return {
        "voltage": bell_draw(part_keys[0], (R, VERTS), 1.0, 4.0, ((1, 32),), jnp.float32),
        "recovery": bell_draw(part_keys[1], (R, VERTS), 0.5, 3.0, ((1, 32),), jnp.float32),
        "increments": bell_draw(part_keys[2], (STEPS, R, VERTS), 1.0, 6.0, ((2, 32),), jnp.float32),
        "band_weight": bell_draw(key_list[3], (VERTS, TILE_V + 2 * HW), (2 * HW) ** -0.5, 0.125, ((0, 32),)),
        "time_scale": jnp.clip(jnp.exp(math.log(0.5) - 2.3025851 * jax.random.uniform(key_list[4], (VERTS,), jnp.float32) ** block_scale(key_list[4], (VERTS,), ((0, 32),), -0.2, 0.2)), 0.05, 0.5),
        "tract_in": bell_draw(key_list[5], (MATCH, VERTS, RANK), RANK ** -0.5, 0.375, ((1, 32),)),
        "tract_out": bell_draw(key_list[6], (MATCH, VERTS, RANK), TILE_V ** -0.5, 0.1875, ((1, 32),)),
        "matching_masks": draw_matching_masks(jax.random.fold_in(key_list[9], 71), part),
        "tract_on": with_ends((jax.random.randint(key_list[8], (TILES, MATCH), 0, 4) < 3).astype(jnp.int32), jax.random.fold_in(key_list[8], 1), 0, 1),
    }


time_step = 0.1
noise_gain = 0.5
shift_a = 0.7
damp_b = 0.8
drive_level = 0.5
band_gain = 1.0
tract_gain = 0.5

def reference(voltage, recovery, increments, band_weight, time_scale, tract_in, tract_out, matching_masks, tract_on):
    window_width = TILE_V + 2 * HW
    row_index = jnp.arange(TILE_V, dtype=jnp.int32)[:, None]
    col_index = jnp.arange(window_width, dtype=jnp.int32)[None, :]
    inband = (col_index - row_index >= 0) & (col_index - row_index <= 2 * HW)
    banded = jnp.where(inband[None], band_weight.reshape(TILES, TILE_V, window_width), jnp.zeros((), jnp.bfloat16))
    partner = jnp.bitwise_xor(jnp.arange(TILES, dtype=jnp.int32)[:, None], matching_masks[None, :])
    gate_float = tract_on.astype(jnp.float32)
    in_tiles = tract_in.reshape(MATCH, TILES, TILE_V, RANK).astype(jnp.float32)
    out_tiles = tract_out.reshape(MATCH, TILES, TILE_V, RANK).astype(jnp.float32)
    match_index = jnp.arange(MATCH, dtype=jnp.int32)[None, :]

    def advance(state_pair, kick_now):
        voltage_now, recovery_now = state_pair
        rounded = voltage_now.astype(jnp.bfloat16)
        padded = jnp.pad(rounded, ((0, 0), (HW, HW)))

        def tile_band(tile_at):
            window = lax.dynamic_slice_in_dim(padded, (tile_at * TILE_V).astype(jnp.int32), window_width, 1)
            return jnp.dot(window, banded[tile_at].T, preferred_element_type=jnp.float32)
        band_drive = lax.map(tile_band, jnp.arange(TILES, dtype=jnp.int32))
        band_drive = band_drive.transpose(1, 0, 2).reshape(R, VERTS)
        projected = jnp.einsum('rtv,mtvk->tmrk', rounded.reshape(R, TILES, TILE_V).astype(jnp.float32), out_tiles).astype(jnp.bfloat16)
        received = projected[partner, match_index].astype(jnp.float32) * gate_float[:, :, None, None]
        tract_drive = jnp.einsum('tmrk,mtvk->rtv', received, in_tiles).reshape(R, VERTS)
        total_drive = band_gain * band_drive + tract_gain * tract_drive + drive_level
        voltage_new = voltage_now + time_step * (voltage_now - voltage_now ** 3 / 3.0 - recovery_now + total_drive) + noise_gain * math.sqrt(time_step) * kick_now
        recovery_new = recovery_now + time_step * time_scale[None, :] * (voltage_now + shift_a - damp_b * recovery_now)
        return ((voltage_new, recovery_new), None)
    (voltage_end, recovery_end), unused = lax.scan(advance, (voltage, recovery), increments)
    return (voltage_end, recovery_end)
```

```python
import functools
import math

import jax
import jax.numpy as jnp
from jax import lax
from jax.experimental import pallas as pl
from jax.experimental.pallas import tpu as pltpu
from jax.sharding import PartitionSpec as P

time_step = 0.1
noise_gain = 0.5
shift_a = 0.7
damp_b = 0.8
drive_level = 0.5
band_gain = 1.0
tract_gain = 0.5

MESH = pl.DeviceIdType.MESH
ROW_BLOCK = 256


def contract_last(left, right):
    return lax.dot_general(
        left, right, (((1,), (1,)), ((), ())), preferred_element_type=jnp.float32
    )


def field_kernel(
    tile_count,
    masks_ref,
    gate_ref,
    v_in,
    w_in,
    scale_in,
    kick_hbm,
    band_hbm,
    tin_hbm,
    tout_hbm,
    v_ref,
    w_ref,
    band,
    tin,
    tout,
    kicks,
    vb,
    left,
    right,
    acc,
    snd,
    rbuf,
    load_sem,
    halo_send,
    halo_recv,
    blk_send,
    blk_recv,
):
    steps = kicks.shape[0]
    match = tin.shape[0]
    rows, cols = v_in.shape
    hw = left.shape[2]
    blocks = cols // ROW_BLOCK
    span = band.shape[2]
    bits = tile_count.bit_length() - 1
    me = lax.axis_index("tile")

    def partner(bit):
        unit = 1 << bit
        return me + unit - 2 * unit * (lax.rem(me // unit, 2))

    loads_out = [
        pltpu.make_async_copy(tout_hbm.at[m], tout.at[m], load_sem.at[m]) for m in range(match)
    ]
    loads_band = [
        pltpu.make_async_copy(
            band_hbm.at[pl.ds(n * ROW_BLOCK, ROW_BLOCK), pl.ds(n * ROW_BLOCK, span)],
            band.at[n],
            load_sem.at[match + n],
        )
        for n in range(blocks)
    ]
    load_in = pltpu.make_async_copy(tin_hbm, tin, load_sem.at[match + blocks])
    load_kick = pltpu.make_async_copy(kick_hbm, kicks, load_sem.at[match + blocks + 1])
    for copy in loads_out + loads_band + [load_in, load_kick]:
        copy.start()

    has_left = me > 0
    has_right = me < tile_count - 1

    barrier = pltpu.get_barrier_semaphore()
    for bit in range(bits):
        pl.semaphore_signal(barrier, inc=1, device_id={"tile": partner(bit)}, device_id_type=MESH)

    @pl.when(has_left)
    def _():
        pl.semaphore_signal(barrier, inc=1, device_id={"tile": me - 1}, device_id_type=MESH)

    @pl.when(has_right)
    def _():
        pl.semaphore_signal(barrier, inc=1, device_id={"tile": me + 1}, device_id_type=MESH)

    v_ref[...] = v_in[...]
    w_ref[...] = w_in[...]

    @pl.when(me == 0)
    def _():
        left[...] = jnp.zeros_like(left)

    @pl.when(me == tile_count - 1)
    def _():
        right[...] = jnp.zeros_like(right)

    for copy in loads_out + loads_band + [load_in, load_kick]:
        copy.wait()
    row = lax.broadcasted_iota(jnp.int32, (ROW_BLOCK, ROW_BLOCK), 0)
    col = lax.broadcasted_iota(jnp.int32, (ROW_BLOCK, ROW_BLOCK), 1)
    for n in range(blocks):
        head = band[n, :, :ROW_BLOCK].astype(jnp.float32)
        band[n, :, :ROW_BLOCK] = jnp.where(col >= row, head, 0.0).astype(jnp.bfloat16)
        tail = band[n, :, span - ROW_BLOCK :].astype(jnp.float32)
        band[n, :, span - ROW_BLOCK :] = jnp.where(col <= row, tail, 0.0).astype(jnp.bfloat16)

    neighbours = bits + jnp.where(has_left, 1, 0) + jnp.where(has_right, 1, 0)
    pl.semaphore_wait(barrier, neighbours)

    def send_left(slot):
        return pltpu.make_async_remote_copy(
            src_ref=vb,
            dst_ref=right.at[slot],
            send_sem=halo_send.at[0],
            recv_sem=halo_recv.at[1, slot],
            device_id={"tile": me - 1},
            device_id_type=MESH,
        )

    def send_right(slot):
        return pltpu.make_async_remote_copy(
            src_ref=vb,
            dst_ref=left.at[slot],
            send_sem=halo_send.at[1],
            recv_sem=halo_recv.at[0, slot],
            device_id={"tile": me + 1},
            device_id_type=MESH,
        )

    def block_copy(slot, turn, m):
        return pltpu.make_async_remote_copy(
            src_ref=snd.at[turn, m],
            dst_ref=rbuf.at[slot, turn, m],
            send_sem=blk_send.at[turn, m],
            recv_sem=blk_recv.at[slot, turn, m],
            device_id={"tile": partner((turn + m) % bits)},
            device_id_type=MESH,
        )

    def own_band(n):
        start = hw - n * ROW_BLOCK
        acc[:, n * ROW_BLOCK : (n + 1) * ROW_BLOCK] = contract_last(
            vb[...], band[n, :, start : start + cols]
        )

    def halo_band(n, slot):
        low = hw - n * ROW_BLOCK
        high = (n + 1) * ROW_BLOCK
        where = slice(n * ROW_BLOCK, (n + 1) * ROW_BLOCK)
        acc[:, where] = (
            acc[:, where]
            + contract_last(left[slot, :, n * ROW_BLOCK :], band[n, :, :low])
            + contract_last(right[slot, :, :high], band[n, :, span - high :])
        )

    def step(at, carry):
        slot = lax.rem(at, 2)
        vb[...] = v_ref[...].astype(jnp.bfloat16)

        @pl.when(has_left)
        def _():
            send_left(slot).start()

        @pl.when(has_right)
        def _():
            send_right(slot).start()

        for m in range(match):
            snd[0, m] = jnp.dot(
                vb[...], tout[m], preferred_element_type=jnp.float32
            ).astype(jnp.bfloat16)
            block_copy(slot, 0, m).start()
        arrived = [None] * match
        for turn in range(bits):
            if turn == 0:
                for n in range(blocks):
                    own_band(n)
            if turn == 1:

                @pl.when(has_left)
                def _():
                    send_right(slot).wait_recv()

                @pl.when(has_right)
                def _():
                    send_left(slot).wait_recv()

                for n in range(blocks):
                    halo_band(n, slot)
            for m in range(match):
                block_copy(slot, turn, m).wait_recv()
                bit = (turn + m) % bits
                chosen = ((masks_ref[m] // (1 << bit)) % 2) == 1
                kept = jnp.where(chosen, rbuf[slot, turn, m], snd[turn, m])
                if turn < bits - 1:
                    snd[turn + 1, m] = kept
                    block_copy(slot, turn + 1, m).start()
                else:
                    arrived[m] = kept * gate_ref[0, m].astype(jnp.float32).astype(jnp.bfloat16)
        tract = contract_last(arrived[0], tin[0])
        for m in range(1, match):
            tract = tract + contract_last(arrived[m], tin[m])
        v = v_ref[...]
        w = w_ref[...]
        total = band_gain * acc[...] + tract_gain * tract + drive_level
        v_ref[...] = (
            v
            + time_step * (v - v * v * v / 3.0 - w + total)
            + noise_gain * math.sqrt(time_step) * kicks[at]
        )
        w_ref[...] = w + time_step * scale_in[...] * (v + shift_a - damp_b * w)

        @pl.when(has_left)
        def _():
            send_left(slot).wait_send()

        @pl.when(has_right)
        def _():
            send_right(slot).wait_send()

        for turn in range(bits):
            for m in range(match):
                block_copy(slot, turn, m).wait_send()
        return carry

    lax.fori_loop(0, steps, step, 0)


def per_device(
    voltage,
    recovery,
    increments,
    band_weight,
    time_scale,
    tract_in,
    tract_out,
    matching_masks,
    tract_on,
):
    tile_count = lax.axis_size("tile")
    bits = tile_count.bit_length() - 1
    rows, cols = voltage.shape
    steps = increments.shape[0]
    match, _, rank = tract_in.shape
    hw = (band_weight.shape[1] - cols) // 2
    blocks = cols // ROW_BLOCK
    span = 2 * hw + ROW_BLOCK
    vmem = pl.BlockSpec(memory_space=pltpu.VMEM)
    smem = pl.BlockSpec(memory_space=pltpu.SMEM)
    hbm = pl.BlockSpec(memory_space=pl.ANY)
    shape = jax.ShapeDtypeStruct((rows, cols), jnp.float32)
    return pl.pallas_call(
        functools.partial(field_kernel, tile_count),
        out_shape=(shape, shape),
        in_specs=[smem, smem, vmem, vmem, vmem, hbm, hbm, hbm, hbm],
        out_specs=(vmem, vmem),
        scratch_shapes=[
            pltpu.VMEM((blocks, ROW_BLOCK, span), jnp.bfloat16),
            pltpu.VMEM((match, cols, rank), jnp.bfloat16),
            pltpu.VMEM((match, cols, rank), jnp.bfloat16),
            pltpu.VMEM((steps, rows, cols), jnp.float32),
            pltpu.VMEM((rows, cols), jnp.bfloat16),
            pltpu.VMEM((2, rows, hw), jnp.bfloat16),
            pltpu.VMEM((2, rows, hw), jnp.bfloat16),
            pltpu.VMEM((rows, cols), jnp.float32),
            pltpu.VMEM((bits, match, rows, rank), jnp.bfloat16),
            pltpu.VMEM((2, bits, match, rows, rank), jnp.bfloat16),
            pltpu.SemaphoreType.DMA((match + blocks + 2,)),
            pltpu.SemaphoreType.DMA((2,)),
            pltpu.SemaphoreType.DMA((2, 2)),
            pltpu.SemaphoreType.DMA((bits, match)),
            pltpu.SemaphoreType.DMA((2, bits, match)),
        ],
        compiler_params=pltpu.CompilerParams(
            collective_id=0, has_side_effects=True, vmem_limit_bytes=50 * 1024 * 1024
        ),
    )(
        matching_masks,
        tract_on,
        voltage,
        recovery,
        time_scale[None, :],
        increments,
        band_weight,
        tract_in,
        tract_out,
    )


def solution(mesh):
    placed = (
        P("real", "tile"),
        P("real", "tile"),
        P(None, "real", "tile"),
        P("tile", None),
        P("tile"),
        P(None, "tile", None),
        P(None, "tile", None),
        P(),
        P("tile", None),
    )
    return jax.shard_map(
        per_device,
        mesh=mesh,
        in_specs=placed,
        out_specs=(P("real", "tile"), P("real", "tile")),
        check_vma=False,
    )
```

```python
import functools
import math

import jax
import jax.numpy as jnp
from jax import lax
from jax.experimental import pallas as pl
from jax.experimental.pallas import tpu as pltpu
from jax.sharding import PartitionSpec as P

time_step = 0.1
noise_gain = 0.5
shift_a = 0.7
damp_b = 0.8
drive_level = 0.5
band_gain = 1.0
tract_gain = 0.5

MESH = pl.DeviceIdType.MESH
ROW_BLOCK = 256


def contract_last(left, right):
    return lax.dot_general(
        left, right, (((1,), (1,)), ((), ())), preferred_element_type=jnp.float32
    )


def field_kernel(
    tile_count,
    cap,
    masks_ref,
    gate_ref,
    v_in,
    w_in,
    scale_in,
    kick_hbm,
    band_hbm,
    tin_hbm,
    tout_hbm,
    v_ref,
    w_ref,
    band,
    tin,
    tout,
    kicks,
    vb,
    left,
    right,
    acc,
    blk,
    snd,
    rbuf,
    load_sem,
    halo_send,
    halo_recv,
    blk_send,
    blk_recv,
):
    steps = kicks.shape[0]
    match = tin.shape[0]
    rows, cols = v_in.shape
    hw = left.shape[2]
    blocks = cols // ROW_BLOCK
    span = band.shape[2]
    bits = tile_count.bit_length() - 1
    me = lax.axis_index("tile")

    low_bits = bits // 2 + bits % 2
    low_count = 1 << low_bits
    high_count = 1 << (bits - low_bits)
    offsets = list(range(1, low_count)) + [h << low_bits for h in range(1, high_count)]
    slots = len(offsets) * cap

    def partner(offset):
        there = me
        for bit in range(bits):
            if (offset >> bit) & 1:
                unit = 1 << bit
                there = there + unit - 2 * unit * lax.rem(me // unit, 2)
        return there

    def as_int(flag):
        return jnp.where(flag, 1, 0)

    masks = [masks_ref[m] for m in range(match)]
    lows = [mask % low_count for mask in masks]
    highs = [mask // low_count for mask in masks]
    clash = {}
    for m in range(match):
        for n in range(m):
            clash[n, m] = as_int((lows[m] == lows[n]) & (lows[m] != 0)) + as_int(
                (highs[m] == highs[n]) & (highs[m] != 0)
            )
    best = None
    for pattern in range(1 << (match - 1)):
        cost = 0
        for (n, m), value in clash.items():
            if ((pattern >> n) & 1) == ((pattern >> m) & 1):
                cost = cost + value
        key = cost * (1 << match) + pattern
        best = key if best is None else jnp.minimum(best, key)
    turns = [(best // (1 << m)) % 2 for m in range(match)]
    route = []
    for rnd in range(2):
        keys = []
        for m in range(match):
            low_key = jnp.where(lows[m] == 0, -1, lows[m] - 1)
            high_key = jnp.where(highs[m] == 0, -1, highs[m] + low_count - 2)
            keys.append(jnp.where(turns[m] == rnd, low_key, high_key))
        places = []
        for m in range(match):
            earlier = 0
            for n in range(m):
                earlier = earlier + as_int(keys[n] == keys[m])
            places.append(jnp.where(keys[m] < 0, -1, keys[m] * cap + earlier))
        route.append(places)
    gates = [gate_ref[0, m] != 0 for m in range(match)]

    loads_out = [
        pltpu.make_async_copy(tout_hbm.at[m], tout.at[m], load_sem.at[m]) for m in range(match)
    ]
    loads_band = [
        pltpu.make_async_copy(
            band_hbm.at[pl.ds(n * ROW_BLOCK, ROW_BLOCK), pl.ds(n * ROW_BLOCK, span)],
            band.at[n],
            load_sem.at[match + n],
        )
        for n in range(blocks)
    ]
    load_in = pltpu.make_async_copy(tin_hbm, tin, load_sem.at[match + blocks])
    load_kick = pltpu.make_async_copy(kick_hbm, kicks, load_sem.at[match + blocks + 1])
    for copy in loads_out + loads_band + [load_in, load_kick]:
        copy.start()

    has_left = me > 0
    has_right = me < tile_count - 1

    barrier = pltpu.get_barrier_semaphore()
    for offset in offsets:
        pl.semaphore_signal(
            barrier, inc=1, device_id={"tile": partner(offset)}, device_id_type=MESH
        )

    @pl.when(has_left)
    def _():
        pl.semaphore_signal(barrier, inc=1, device_id={"tile": me - 1}, device_id_type=MESH)

    @pl.when(has_right)
    def _():
        pl.semaphore_signal(barrier, inc=1, device_id={"tile": me + 1}, device_id_type=MESH)

    v_ref[...] = v_in[...]
    w_ref[...] = w_in[...]

    @pl.when(me == 0)
    def _():
        left[...] = jnp.zeros_like(left)

    @pl.when(me == tile_count - 1)
    def _():
        right[...] = jnp.zeros_like(right)

    def mask_band():
        row = lax.broadcasted_iota(jnp.int32, (ROW_BLOCK, ROW_BLOCK), 0)
        col = lax.broadcasted_iota(jnp.int32, (ROW_BLOCK, ROW_BLOCK), 1)
        for n in range(blocks):
            head = band[n, :, :ROW_BLOCK].astype(jnp.float32)
            band[n, :, :ROW_BLOCK] = jnp.where(col >= row, head, 0.0).astype(jnp.bfloat16)
            tail = band[n, :, span - ROW_BLOCK :].astype(jnp.float32)
            band[n, :, span - ROW_BLOCK :] = jnp.where(col <= row, tail, 0.0).astype(
                jnp.bfloat16
            )

    neighbours = len(offsets) + jnp.where(has_left, 1, 0) + jnp.where(has_right, 1, 0)
    pl.semaphore_wait(barrier, neighbours)

    def send_left(slot):
        return pltpu.make_async_remote_copy(
            src_ref=vb,
            dst_ref=right.at[slot],
            send_sem=halo_send.at[0],
            recv_sem=halo_recv.at[1, slot],
            device_id={"tile": me - 1},
            device_id_type=MESH,
        )

    def send_right(slot):
        return pltpu.make_async_remote_copy(
            src_ref=vb,
            dst_ref=left.at[slot],
            send_sem=halo_send.at[1],
            recv_sem=halo_recv.at[0, slot],
            device_id={"tile": me + 1},
            device_id_type=MESH,
        )

    def block_copy(slot, rnd, q):
        return pltpu.make_async_remote_copy(
            src_ref=snd.at[rnd, q],
            dst_ref=rbuf.at[slot, rnd, q],
            send_sem=blk_send.at[rnd, q],
            recv_sem=blk_recv.at[slot, rnd, q],
            device_id={"tile": partner(offsets[q // cap])},
            device_id_type=MESH,
        )

    def send_blocks(slot, rnd):
        for q in range(slots):
            chosen = blk[rnd, match - 1]
            for m in range(match - 1):
                chosen = jnp.where(route[rnd][m] == q, blk[rnd, m], chosen)
            snd[rnd, q] = chosen
            block_copy(slot, rnd, q).start()

    def take_blocks(slot, rnd):
        for q in range(slots):
            block_copy(slot, rnd, q).wait_recv()
        taken = [blk[rnd, m] for m in range(match)]
        for q in range(slots):
            came = rbuf[slot, rnd, q]
            taken = [
                jnp.where(route[rnd][m] == q, came, taken[m]) for m in range(match)
            ]
        return taken

    def own_band(n):
        start = hw - n * ROW_BLOCK
        acc[:, n * ROW_BLOCK : (n + 1) * ROW_BLOCK] = contract_last(
            vb[...], band[n, :, start : start + cols]
        )

    def halo_band(n, slot):
        low = hw - n * ROW_BLOCK
        high = (n + 1) * ROW_BLOCK
        where = slice(n * ROW_BLOCK, (n + 1) * ROW_BLOCK)
        acc[:, where] = (
            acc[:, where]
            + contract_last(left[slot, :, n * ROW_BLOCK :], band[n, :, :low])
            + contract_last(right[slot, :, :high], band[n, :, span - high :])
        )

    def step(at, carry):
        slot = lax.rem(at, 2)
        vb[...] = v_ref[...].astype(jnp.bfloat16)

        @pl.when(has_left)
        def _():
            send_left(slot).start()

        @pl.when(has_right)
        def _():
            send_right(slot).start()

        @pl.when(at == 0)
        def _():
            for copy in loads_out:
                copy.wait()

        for m in range(match):
            blk[0, m] = jnp.dot(
                vb[...], tout[m], preferred_element_type=jnp.float32
            ).astype(jnp.bfloat16)
        send_blocks(slot, 0)

        @pl.when(at == 0)
        def _():
            for copy in loads_band + [load_in, load_kick]:
                copy.wait()
            mask_band()

        for n in range(blocks):
            own_band(n)
        taken = take_blocks(slot, 0)
        for m in range(match):
            blk[1, m] = taken[m]
        send_blocks(slot, 1)

        @pl.when(has_left)
        def _():
            send_right(slot).wait_recv()

        @pl.when(has_right)
        def _():
            send_left(slot).wait_recv()

        for n in range(blocks):
            halo_band(n, slot)
        arrived = [
            jnp.where(gates[m], block, jnp.zeros_like(block))
            for m, block in enumerate(take_blocks(slot, 1))
        ]
        tract = contract_last(arrived[0], tin[0])
        for m in range(1, match):
            tract = tract + contract_last(arrived[m], tin[m])
        v = v_ref[...]
        w = w_ref[...]
        total = band_gain * acc[...] + tract_gain * tract + drive_level
        v_ref[...] = (
            v
            + time_step * (v - v * v * v / 3.0 - w + total)
            + noise_gain * math.sqrt(time_step) * kicks[at]
        )
        w_ref[...] = w + time_step * scale_in[...] * (v + shift_a - damp_b * w)

        @pl.when(has_left)
        def _():
            send_left(slot).wait_send()

        @pl.when(has_right)
        def _():
            send_right(slot).wait_send()

        for rnd in range(2):
            for q in range(slots):
                block_copy(slot, rnd, q).wait_send()
        return carry

    lax.fori_loop(0, steps, step, 0)


def per_device(
    voltage,
    recovery,
    increments,
    band_weight,
    time_scale,
    tract_in,
    tract_out,
    matching_masks,
    tract_on,
):
    tile_count = lax.axis_size("tile")
    bits = tile_count.bit_length() - 1
    low_bits = bits // 2 + bits % 2
    low_count = 1 << low_bits
    high_count = 1 << (bits - low_bits)
    rows, cols = voltage.shape
    steps = increments.shape[0]
    match, _, rank = tract_in.shape
    hw = (band_weight.shape[1] - cols) // 2
    blocks = cols // ROW_BLOCK
    span = 2 * hw + ROW_BLOCK
    vmem = pl.BlockSpec(memory_space=pltpu.VMEM)
    smem = pl.BlockSpec(memory_space=pltpu.SMEM)
    hbm = pl.BlockSpec(memory_space=pl.ANY)
    shape = jax.ShapeDtypeStruct((rows, cols), jnp.float32)

    def run(cap, *operands):
        slots = cap * (low_count + high_count - 2)
        return pl.pallas_call(
            functools.partial(field_kernel, tile_count, cap),
            out_shape=(shape, shape),
            in_specs=[smem, smem, vmem, vmem, vmem, hbm, hbm, hbm, hbm],
            out_specs=(vmem, vmem),
            scratch_shapes=[
                pltpu.VMEM((blocks, ROW_BLOCK, span), jnp.bfloat16),
                pltpu.VMEM((match, cols, rank), jnp.bfloat16),
                pltpu.VMEM((match, cols, rank), jnp.bfloat16),
                pltpu.VMEM((steps, rows, cols), jnp.float32),
                pltpu.VMEM((rows, cols), jnp.bfloat16),
                pltpu.VMEM((2, rows, hw), jnp.bfloat16),
                pltpu.VMEM((2, rows, hw), jnp.bfloat16),
                pltpu.VMEM((rows, cols), jnp.float32),
                pltpu.VMEM((2, match, rows, rank), jnp.bfloat16),
                pltpu.VMEM((2, slots, rows, rank), jnp.bfloat16),
                pltpu.VMEM((2, 2, slots, rows, rank), jnp.bfloat16),
                pltpu.SemaphoreType.DMA((match + blocks + 2,)),
                pltpu.SemaphoreType.DMA((2,)),
                pltpu.SemaphoreType.DMA((2, 2)),
                pltpu.SemaphoreType.DMA((2, slots)),
                pltpu.SemaphoreType.DMA((2, 2, slots)),
            ],
            compiler_params=pltpu.CompilerParams(
                collective_id=cap, has_side_effects=True, vmem_limit_bytes=50 * 1024 * 1024
            ),
        )(*operands)

    masks = [matching_masks[m] for m in range(match)]
    crowded = jnp.zeros((), jnp.bool_)
    for one in range(match):
        for two in range(one):
            for three in range(two):
                for part in (lambda k: k & (low_count - 1), lambda k: k >> low_bits):
                    first = part(masks[one])
                    crowded = crowded | (
                        (first != 0)
                        & (first == part(masks[two]))
                        & (first == part(masks[three]))
                    )
    return lax.cond(
        crowded,
        functools.partial(run, (match + 1) // 2),
        functools.partial(run, 1),
        matching_masks,
        tract_on,
        voltage,
        recovery,
        time_scale[None, :],
        increments,
        band_weight,
        tract_in,
        tract_out,
    )


def solution(mesh):
    placed = (
        P("real", "tile"),
        P("real", "tile"),
        P(None, "real", "tile"),
        P("tile", None),
        P("tile"),
        P(None, "tile", None),
        P(None, "tile", None),
        P(),
        P("tile", None),
    )
    return jax.shard_map(
        per_device,
        mesh=mesh,
        in_specs=placed,
        out_specs=(P("real", "tile"), P("real", "tile")),
        check_vma=False,
    )
```
